128 devices in a mesh: fsdp: 64 (over z, x_hi, y, core), tp: 2 (over x_lo).
Axes of the slice: x: 4 (x_hi: 2, x_lo: 2; x = x_hi * 2 + x_lo), y: 4, z: 4, core: 2. Of those that a mesh axis runs over, the one named last changes fastest.
Arguments:
- residual_in: bfloat16 [16384, 2048], P(('fsdp', 'tp')), may hold values from -24 to 24
- query_weight: bfloat16 [2048, 2048], P('fsdp', 'tp'), may hold values from -0.125 to 0.125
- key_weight: bfloat16 [2048, 1024], P('fsdp', 'tp'), may hold values from -0.125 to 0.125
- value_weight: bfloat16 [2048, 1024], P('fsdp', 'tp'), may hold values from -0.125 to 0.125
- output_weight: bfloat16 [2048, 2048], P('fsdp', 'tp'), may hold values from -0.75 to 0.75
- gate_weight: bfloat16 [2048, 6144], P('fsdp', 'tp'), may hold values from -0.125 to 0.125
- up_weight: bfloat16 [2048, 6144], P('fsdp', 'tp'), may hold values from -0.125 to 0.125
- down_weight: bfloat16 [2048, 6144], P('fsdp', 'tp'), may hold values from -0.078125 to 0.078125
- input_gain: bfloat16 [2048], P('fsdp'), may hold values from 0.25 to 1.75
- post_gain: bfloat16 [2048], P('fsdp'), may hold values from 0.25 to 1.75
- query_gain: bfloat16 [128], P('fsdp'), may hold values from 0.25 to 1.75
- key_gain: bfloat16 [128], P('fsdp'), may hold values from 0.25 to 1.75
- lengths: int32 [64], P('fsdp'), may hold values from 192 to 256, as said below
- cotangent: bfloat16 [16384, 2048], P(('fsdp', 'tp')), may hold values from -24 to 24
Outputs:
- block_out: bfloat16 [16384, 2048], P(('fsdp', 'tp'))
- input_grad: bfloat16 [16384, 2048], P(('fsdp', 'tp'))
- query_weight_grad: float32 [2048, 2048], P('fsdp', 'tp')
- key_weight_grad: float32 [2048, 1024], P('fsdp', 'tp')
- value_weight_grad: float32 [2048, 1024], P('fsdp', 'tp')
- output_weight_grad: float32 [2048, 2048], P('fsdp', 'tp')
- gate_weight_grad: float32 [2048, 6144], P('fsdp', 'tp')
- up_weight_grad: float32 [2048, 6144], P('fsdp', 'tp')
- down_weight_grad: float32 [2048, 6144], P('fsdp', 'tp')
- input_gain_grad: float32 [2048], P('fsdp')
- post_gain_grad: float32 [2048], P('fsdp')
- query_gain_grad: float32 [128], P('fsdp')
- key_gain_grad: float32 [128], P('fsdp')
The draws below stay inside these ranges and needn't reach their ends.
Inputs may be any that keep to these rules, and one draw needn't show every extreme that they name: `lengths`: each sequence is right-padded; in every draw some sequence is full and some has exactly 192 valid tokens.
All inputs are finite; a program needn't handle non-finite values.
Results may differ from the reference program's by a relative error of at most 0.028.
Values may be sent and summed in bfloat16 or wider, within the bound.
A program may use at most 256 MiB of HBM per device.

```python
import math
import jax
import jax.numpy as jnp
from jax import lax

D = 2048
H = 16
KV = 8
HD = 128
FF = 6144
L = 256
SEQS = 64
TOKENS = 16384


def draw_lengths(key, part):
    key = jax.random.fold_in(key, 11)
    draw_key, pick_key = jax.random.split(key)
    shortest = L - L // 4
    drawn_lengths = jax.random.randint(draw_key, (SEQS,), shortest, L + 1)
    ordering = jax.random.permutation(pick_key, SEQS)
    drawn_lengths = drawn_lengths.at[ordering[0]].set(L)
    drawn_lengths = drawn_lengths.at[ordering[1]].set(shortest)
    return drawn_lengths.astype(jnp.int32)


def with_spikes(values, key, source, target, shards_of, factor):
    owner, partner = [(jnp.arange(values.shape[position]) // (values.shape[position] // shards_of)).reshape([-1 if axis == position else 1 for axis in range(values.ndim)]) for position in (source, target)]
    chosen = jax.random.permutation(key, shards_of)[partner]
    strong = (owner == chosen) | (owner == (partner + shards_of // 2) % shards_of)
    return jnp.where(strong, factor * values, values)


def block_levels(own_key, extent, cuts, smallest, top_value):
    level = 1.0
    for dim, parts in cuts:
        heights = jax.random.uniform(jax.random.fold_in(jax.random.fold_in(own_key, 6), dim), (parts,), jnp.float32, smallest / len(cuts), top_value / len(cuts))
        level = level * jnp.repeat(jnp.exp(heights), extent[dim] // parts).reshape((-1,) + (1,) * (len(extent) - 1 - dim))
    return level


def noise(key, dims, width, bound, shards=(), kind=jnp.bfloat16):
    level = block_levels(key, dims, shards, -0.22, 0.18) if shards else 1.0
    result = jax.random.normal(key, dims, jnp.float32) * width * level
    return jnp.minimum(jnp.maximum(result, -bound), bound).astype(kind)


def bell_draw_with(key, dims, deviation, limit, cuts, heavy, kind=jnp.bfloat16):
    drawn = deviation * jax.random.normal(key, dims, jnp.float32)
    if cuts:
        drawn = drawn * block_levels(key, dims, cuts, -0.22, 0.18)
    return jnp.clip(with_spikes(drawn, jax.random.fold_in(key, 3), *heavy), -limit, limit).astype(kind)


def setup_inputs(seed: int = 0) -> dict:
    seeds = jax.random.split(jax.random.key(seed), 15)
    residual_in = bell_draw_with(seeds[0], (TOKENS, D), 1.0, 24.0, ((0, 128),), (0, 1, 128, 5.5))
    query_weight = noise(seeds[1], (D, H * HD), D ** -0.5, 0.125, ((0, 64), (1, 2)))
    key_weight = noise(seeds[2], (D, KV * HD), D ** -0.5, 0.125, ((0, 64), (1, 2)))
    value_weight = noise(seeds[3], (D, KV * HD), D ** -0.5, 0.125, ((0, 64), (1, 2)))
    output_weight = noise(seeds[4], (D, H * HD), (max(H * HD * 8 // L, 16)) ** -0.5, 0.75, ((0, 64), (1, 2)))
    gate_weight = noise(seeds[5], (D, FF), D ** -0.5, 0.125, ((0, 64), (1, 2)))
    up_weight = noise(seeds[6], (D, FF), D ** -0.5, 0.125, ((0, 64), (1, 2)))
    down_weight = noise(seeds[7], (D, FF), FF ** -0.5, 0.078125, ((0, 64), (1, 2)))
    input_gain = jnp.clip(1.0 + 0.15 * jax.random.normal(seeds[8], (D,), jnp.float32), 0.25, 1.75).astype(jnp.bfloat16)
    post_gain = jnp.clip(1.0 + 0.15 * jax.random.normal(seeds[9], (D,), jnp.float32), 0.25, 1.75).astype(jnp.bfloat16)
    query_gain = jnp.clip(1.0 + 0.15 * jax.random.normal(seeds[10], (HD,), jnp.float32), 0.25, 1.75).astype(jnp.bfloat16)
    key_gain = jnp.clip(1.0 + 0.15 * jax.random.normal(seeds[11], (HD,), jnp.float32), 0.25, 1.75).astype(jnp.bfloat16)
    lengths = draw_lengths(jax.random.fold_in(seeds[14], 71), 0)
    cotangent = bell_draw_with(seeds[13], (TOKENS, D), 1.0, 24.0, ((0, 128),), (0, 1, 128, 5.5))
    return {"residual_in": residual_in, "query_weight": query_weight, "key_weight": key_weight, "value_weight": value_weight, "output_weight": output_weight, "gate_weight": gate_weight, "up_weight": up_weight, "down_weight": down_weight, "input_gain": input_gain, "post_gain": post_gain, "query_gain": query_gain, "key_gain": key_gain, "lengths": lengths, "cotangent": cotangent}


@jax.custom_vjp
def low(v):
    return lax.optimization_barrier(v.astype(jnp.bfloat16)).astype(jnp.float32)

@jax.custom_vjp
def low_back(v):
    return v

def low_keep(v):
    return (low(v), None)

def low_pass(kept, grad):
    return (grad,)

def back_keep(v):
    return (v, None)

def back_low(kept, grad):
    return (low(grad),)
low.defvjp(low_keep, low_pass)
low_back.defvjp(back_keep, back_low)
EPSILON = 1e-06
THETA = 1000000.0

def norm_scale(values, gain):
    return values * lax.rsqrt(lax.optimization_barrier(jnp.mean(values * values, axis=-1, keepdims=True)) + EPSILON) * gain

def rotary(values, positions):
    half_size = values.shape[-1] // 2
    frequency = THETA ** (-2.0 * jnp.arange(half_size, dtype=jnp.float32) / values.shape[-1])
    angles = positions[:, None] * frequency[None, :]
    angles = jnp.concatenate([angles, angles], axis=-1)[:, None, :]
    rotated = jnp.concatenate([-values[..., half_size:], values[..., :half_size]], axis=-1)
    return values * jnp.cos(angles) + rotated * jnp.sin(angles)

def prepare(projected, gain, positions):
    head_size = gain.shape[0]
    shaped = projected.reshape(projected.shape[:-1] + (projected.shape[-1] // head_size, head_size))
    return rotary(norm_scale(shaped, gain), positions)

def product(form, left_side, right_side):
    return jnp.einsum(form, left_side, right_side, precision=lax.Precision.HIGHEST)

def decoder(inputs, spans, params):
    query_weight, key_weight, value_weight, output_weight, gate_weight, up_weight, down_weight, input_gain, post_gain, query_gain, key_gain = params
    group_size = inputs.shape[0]
    positions = jnp.arange(L, dtype=jnp.float32)
    normed_one = low(norm_scale(inputs, input_gain))
    query_proj = low_back(product('bld,de->ble', normed_one, query_weight))
    key_proj = low_back(product('bld,de->ble', normed_one, key_weight))
    value_proj = low(low_back(product('bld,de->ble', normed_one, value_weight)))
    query_rot = low(prepare(query_proj, query_gain, positions))
    key_rot = low(prepare(key_proj, key_gain, positions))
    value_heads = value_proj.reshape(group_size, L, KV, HD)
    query_groups = query_rot.reshape(group_size, L, KV, H // KV, HD)
    scores = low_back(product('bqgrd,bkgd->bgrqk', query_groups, key_rot) * HD ** (-0.5))
    places = jnp.arange(L, dtype=jnp.int32)
    causal = places[None, :] <= places[:, None]
    allowed = causal[None, :, :] & (places[None, None, :] < spans[:, None, None])
    allowed = allowed[:, None, None, :, :]
    masked = jnp.where(allowed, scores, -1e+30)
    row_max = lax.optimization_barrier(jnp.max(masked, axis=-1, keepdims=True))
    weights_exp = jnp.exp(masked - row_max)
    probabilities = weights_exp / lax.optimization_barrier(jnp.sum(weights_exp, axis=-1, keepdims=True))
    mixed = product('bgrqk,bkgd->bqgrd', low(probabilities), value_heads)
    attended = low_back(low(mixed.reshape(group_size, L, H * HD)))
    projected = low_back(product('ble,de->bld', attended, output_weight))
    middle = inputs + projected
    normed_two = low(norm_scale(middle, post_gain))
    gate_proj = low_back(product('bld,df->blf', normed_two, gate_weight))
    up_proj = low_back(product('bld,df->blf', normed_two, up_weight))
    hidden_units = low(jax.nn.silu(gate_proj) * up_proj)
    return middle + low_back(product('blf,df->bld', hidden_units, down_weight))

def reference(residual_in, query_weight, key_weight, value_weight, output_weight, gate_weight, up_weight, down_weight, input_gain, post_gain, query_gain, key_gain, lengths, cotangent):
    weights = (query_weight, key_weight, value_weight, output_weight, gate_weight, up_weight, down_weight, input_gain, post_gain, query_gain, key_gain)
    params = tuple((entry.astype(jnp.float32) for entry in weights))
    group_size = math.gcd(SEQS, max(1, 4096 // L))
    steps_count = SEQS // group_size
    inputs = residual_in.astype(jnp.float32).reshape(steps_count, group_size, L, D)
    cotangents = cotangent.astype(jnp.float32).reshape(steps_count, group_size, L, D)
    spans = lengths.astype(jnp.int32).reshape(steps_count, group_size)

    def sequence_step(totals, scanned):
        block_in, block_cot, block_len = scanned
        keep_rows = (jnp.arange(L, dtype=jnp.int32)[None, :] < block_len[:, None]).astype(jnp.float32)
        outputs, pullback = jax.vjp(lambda inner, weights_in: decoder(inner, block_len, weights_in), block_in, params)
        grad_in, weight_grads = pullback(block_cot * keep_rows[:, :, None])
        totals = jax.tree.map(lambda acc_value, new_value: acc_value + new_value, totals, weight_grads)
        return (totals, (outputs, grad_in))
    initial = jax.tree.map(jnp.zeros_like, params)
    totals, (outputs, grads_in) = lax.scan(sequence_step, initial, (inputs, cotangents, spans))
    return (outputs.reshape(TOKENS, D).astype(jnp.bfloat16), grads_in.reshape(TOKENS, D).astype(jnp.bfloat16), totals[0], totals[1], totals[2], totals[3], totals[4], totals[5], totals[6], totals[7], totals[8], totals[9], totals[10])
```

```python
import functools

import jax
import jax.numpy as jnp
from jax import lax
from jax.experimental import pallas as pl
from jax.experimental.pallas import tpu as pltpu
from jax.sharding import PartitionSpec as P

EPSILON = 1e-06
THETA = 1000000.0
MESH = pl.DeviceIdType.MESH
F32 = jnp.float32
BF16 = jnp.bfloat16
ROWS = 128
WIDTH = 2048
GATHER_COLS = (640, 256, 1536, 768)
SCATTER_COLS = (768, 1536, 256, 512)


class Place:
    def __init__(self):
        index = lax.axis_index("fsdp")
        self.t = lax.axis_index("tp")
        self.c = lax.rem(index, 2)
        self.y = lax.rem(lax.div(index, 2), 4)
        self.xh = lax.rem(lax.div(index, 8), 2)
        self.z = lax.div(index, 16)
        self.x = self.xh * 2 + self.t

    def device(self, x=0, y=0, z=0, c=0):
        ax = lax.rem(self.x + x, 4) if x else self.x
        ay = lax.rem(self.y + y, 4) if y else self.y
        az = lax.rem(self.z + z, 4) if z else self.z
        ac = 1 - self.c if c else self.c
        return (((az * 2 + lax.div(ax, 2)) * 4 + ay) * 2 + ac, lax.rem(ax, 2))


class Copies:
    def __init__(self, send_sems, recv_sems):
        self.send_sems, self.recv_sems = send_sems, recv_sems
        self.used = 0
        self.open = []

    def send(self, source, target, device):
        copy = pltpu.make_async_remote_copy(
            src_ref=source,
            dst_ref=target,
            send_sem=self.send_sems.at[self.used],
            recv_sem=self.recv_sems.at[self.used],
            device_id=device,
            device_id_type=MESH,
        )
        copy.start()
        self.used += 1
        self.open.append(copy)
        return copy

    def finish(self):
        for copy in self.open:
            copy.wait_send()
        self.open = []


def greet(devices):
    barrier = pltpu.get_barrier_semaphore()
    for device in devices:
        pl.semaphore_signal(barrier, inc=1, device_id=device, device_id_type=MESH)
    pl.semaphore_wait(barrier, len(devices))


def run_all(jobs):
    jobs = list(jobs)
    while jobs:
        alive = []
        for job in jobs:
            try:
                next(job)
                alive.append(job)
            except StopIteration:
                pass
        jobs = alive


def ring_gather(copies, mine, view, halves, up, down):
    above, below = lax.rem(mine + 1, 4), lax.rem(mine + 3, 4)
    first_up = copies.send(view(mine), view(mine), up)
    first_down = copies.send(view(mine), view(mine), down)
    yield
    first_up.wait_recv()
    half = halves(below)[0]
    second_up = copies.send(half, half, up)
    yield
    first_down.wait_recv()
    half = halves(above)[1]
    second_down = copies.send(half, half, down)
    yield
    second_up.wait_recv()
    yield
    second_down.wait_recv()


def ring_scatter(copies, mine, view, halves, up, down, small, large, add_into):
    above, below, across = (lax.rem(mine + k, 4) for k in (1, 3, 2))
    first_up = copies.send(halves(across)[0], small[0], up)
    first_down = copies.send(halves(across)[1], small[1], down)
    yield
    first_up.wait_recv()
    add_into(halves(above)[0], small[0])
    second_up = copies.send(view(above), large[0], up)
    yield
    first_down.wait_recv()
    add_into(halves(below)[1], small[1])
    second_down = copies.send(view(below), large[1], down)
    yield
    second_up.wait_recv()
    yield
    second_down.wait_recv()


def add_blocks(target, *sources, rows=16):
    shape = target.shape
    depth = shape[-2] // rows
    count = depth
    for extent in shape[:-2]:
        count *= extent

    def step(i, carry):
        rest = lax.div(i, depth)
        index = []
        for extent in reversed(shape[:-2]):
            index.insert(0, lax.rem(rest, extent))
            rest = lax.div(rest, extent)
        index.append(pl.ds(pl.multiple_of(lax.rem(i, depth) * rows, rows), rows))
        index = tuple(index)
        total = target[index].astype(F32)
        for source in sources:
            total = total + source[index].astype(F32)
        target[index] = total.astype(target.dtype)
        return carry

    lax.fori_loop(0, count, step, 0)


def gather_weight(copies, place, packed, full):
    z, xh, y, c = place.z, place.xh, place.y, place.c
    spot = full.at[z, xh, y, c]
    exchanged = [
        copies.send(packed.at[xh * 2 + 1 - c], spot, place.device(c=1)),
        copies.send(packed.at[(1 - xh) * 2 + c], spot, place.device(x=2)),
        copies.send(packed.at[(1 - xh) * 2 + 1 - c], spot, place.device(x=2, c=1)),
    ]
    yield
    for copy in exchanged:
        copy.wait_recv()
    z_up, z_down = place.device(z=1), place.device(z=3)
    y_up, y_down = place.device(y=1), place.device(y=3)
    a_first = ring_gather(
        copies, y, lambda p: full.at[z, 0, p], lambda p: (full.at[z, 0, p, 0], full.at[z, 0, p, 1]), y_up, y_down
    )
    b_first = ring_gather(
        copies, z, lambda p: full.at[p, 1, y], lambda p: (full.at[p, 1, y, 0], full.at[p, 1, y, 1]), z_up, z_down
    )
    a_then = lambda: ring_gather(
        copies, z, lambda p: full.at[p, 0], lambda p: (full.at[p, 0, 0:2], full.at[p, 0, 2:4]), z_up, z_down
    )
    b_then = lambda: ring_gather(
        copies, y, lambda p: full.at[:, 1, p], lambda p: (full.at[0:2, 1, p], full.at[2:4, 1, p]), y_up, y_down
    )
    yield from both(a_first, b_first)
    yield from both(a_then(), b_then())


def both(*jobs):
    jobs = list(jobs)
    while jobs:
        alive = []
        for job in jobs:
            try:
                next(job)
                alive.append(job)
            except StopIteration:
                pass
        jobs = alive
        if jobs:
            yield


def weights_gather_kernel(*refs):
    n = len(GATHER_COLS)
    packed, full = refs[:n], refs[n : 2 * n]
    send_sems, recv_sems, local_sems = refs[2 * n :]
    place = Place()
    own = []
    for k in range(n):
        copy = pltpu.make_async_copy(
            packed[k].at[place.xh * 2 + place.c], full[k].at[place.z, place.xh, place.y, place.c], local_sems.at[k]
        )
        copy.start()
        own.append(copy)
    greet([place.device(**step) for step in WEIGHT_PARTNERS])
    for copy in own:
        copy.wait()
    copies = Copies(send_sems, recv_sems)
    run_all([gather_weight(copies, place, packed[k], full[k]) for k in range(n)])
    copies.finish()


WEIGHT_PARTNERS = (
    dict(c=1),
    dict(x=2),
    dict(x=2, c=1),
    dict(z=1),
    dict(z=3),
    dict(y=1),
    dict(y=3),
)


def weights_gather(packed):
    n = len(packed)
    count = 19 * n
    return pl.pallas_call(
        weights_gather_kernel,
        out_shape=[jax.ShapeDtypeStruct((4, 2, 4, 2, 32, p.shape[-1]), BF16) for p in packed],
        in_specs=[pl.BlockSpec(memory_space=pl.ANY)] * n,
        out_specs=[pl.BlockSpec(memory_space=pl.ANY)] * n,
        scratch_shapes=[
            pltpu.SemaphoreType.DMA((count,)),
            pltpu.SemaphoreType.DMA((count,)),
            pltpu.SemaphoreType.DMA((n,)),
        ],
        compiler_params=pltpu.CompilerParams(collective_id=0, has_side_effects=True),
        name="weights_gather",
    )(*packed)


def scatter_weight(copies, place, full, out, stage, recv, columns):
    z, xh, y, c = place.z, place.xh, place.y, place.c
    small_a, small_b, large_a, large_b, small_c, small_d, large_c, large_d = recv
    z_up, z_down = place.device(z=1), place.device(z=3)
    y_up, y_down = place.device(y=1), place.device(y=3)
    a_first = ring_scatter(
        copies, z,
        lambda p: full.at[p, 0], lambda p: (full.at[p, 0, 0:2], full.at[p, 0, 2:4]),
        z_up, z_down, (small_a.at[0], small_a.at[1]), (large_a.at[0], large_a.at[1]), add_blocks,
    )
    b_first = ring_scatter(
        copies, y,
        lambda p: full.at[:, 1, p], lambda p: (full.at[0:2, 1, p], full.at[2:4, 1, p]),
        y_up, y_down, (small_b.at[0], small_b.at[1]), (large_b.at[0], large_b.at[1]), add_blocks,
    )
    yield from both(a_first, b_first)
    add_blocks(full.at[z, 0], large_a.at[0], large_a.at[1])
    add_blocks(full.at[:, 1, y], large_b.at[0], large_b.at[1])
    a_then = ring_scatter(
        copies, y,
        lambda p: full.at[z, 0, p], lambda p: (full.at[z, 0, p, 0:32], full.at[z, 0, p, 32:64]),
        y_up, y_down, (small_c.at[0], small_c.at[1]), (large_c.at[0], large_c.at[1]), add_blocks,
    )
    b_then = ring_scatter(
        copies, z,
        lambda p: full.at[p, 1, y], lambda p: (full.at[p, 1, y, 0:32], full.at[p, 1, y, 32:64]),
        z_up, z_down, (small_d.at[0], small_d.at[1]), (large_d.at[0], large_d.at[1]), add_blocks,
    )
    yield from both(a_then, b_then)

    def finish(half, large):
        for core in range(2):
            rows = slice(32 * core, 32 * core + 32)
            total = full[z, half, y, rows, :].astype(F32) + large[0, rows, :].astype(F32) + large[1, rows, :].astype(F32)
            stage[half, core] = total.astype(BF16)

    finish(0, large_c)
    finish(1, large_d)
    quarter = xh * 2 + c
    spot = out.at[quarter]
    exchanged = [
        copies.send(stage.at[xh, 1 - c], spot, place.device(c=1)),
        copies.send(stage.at[1 - xh, c], spot, place.device(x=2)),
        copies.send(stage.at[1 - xh, 1 - c], spot, place.device(x=2, c=1)),
    ]
    out[quarter] = stage[xh, c]
    yield
    for copy in exchanged:
        copy.wait_recv()


def weights_scatter_kernel(*refs):
    n = len(SCATTER_COLS)
    given, outs = refs[:n], refs[n : 2 * n]
    full = refs[2 * n : 3 * n]
    stages = refs[3 * n : 4 * n]
    recvs = refs[4 * n : 12 * n]
    send_sems, recv_sems, local_sems = refs[12 * n :]
    place = Place()
    loads = []
    for k in range(n):
        copy = pltpu.make_async_copy(given[k], full[k], local_sems.at[k])
        copy.start()
        loads.append(copy)
    greet([place.device(**step) for step in WEIGHT_PARTNERS])
    copies = Copies(send_sems, recv_sems)
    for copy in loads:
        copy.wait()
    run_all(
        [
            scatter_weight(copies, place, full[k], outs[k], stages[k], recvs[8 * k : 8 * k + 8], SCATTER_COLS[k])
            for k in range(n)
        ]
    )
    copies.finish()


def recv_shapes(n):
    return [
        pltpu.VMEM((2, 2, 4, 64, n), BF16),
        pltpu.VMEM((2, 2, 4, 64, n), BF16),
        pltpu.VMEM((2, 4, 64, n), BF16),
        pltpu.VMEM((2, 4, 64, n), BF16),
    ]


def scatter_scratch(n):
    return [
        pltpu.VMEM((2, 2, 64, n), BF16),
        pltpu.VMEM((2, 2, 64, n), BF16),
        pltpu.VMEM((2, 4, 64, n), BF16),
        pltpu.VMEM((2, 4, 64, n), BF16),
        pltpu.VMEM((2, 32, n), BF16),
        pltpu.VMEM((2, 32, n), BF16),
        pltpu.VMEM((2, 64, n), BF16),
        pltpu.VMEM((2, 64, n), BF16),
    ]


def weights_scatter(given):
    n = len(given)
    count = 19 * n
    scratch = [pltpu.VMEM((4, 2, 4, 64, g.shape[-1]), BF16) for g in given]
    scratch += [pltpu.VMEM((2, 2, 32, g.shape[-1]), BF16) for g in given]
    for g in given:
        scratch += scatter_scratch(g.shape[-1])
    scratch += [
        pltpu.SemaphoreType.DMA((count,)),
        pltpu.SemaphoreType.DMA((count,)),
        pltpu.SemaphoreType.DMA((n,)),
    ]
    return pl.pallas_call(
        weights_scatter_kernel,
        out_shape=[jax.ShapeDtypeStruct((4, 32, g.shape[-1]), BF16) for g in given],
        in_specs=[pl.BlockSpec(memory_space=pl.ANY)] * n,
        out_specs=[pl.BlockSpec(memory_space=pltpu.VMEM)] * n,
        scratch_shapes=scratch,
        compiler_params=pltpu.CompilerParams(
            collective_id=1, has_side_effects=True, vmem_limit_bytes=56 * 2**20
        ),
        name="weights_scatter",
    )(*[g.reshape(4, 2, 4, 64, g.shape[-1]) for g in given])


def gather_tokens_job(copies, place, tokens):
    c = place.c

    def view(x):
        return tokens.at[lax.div(x, 2), c, lax.rem(x, 2)]

    up, down, sibling = place.device(x=1), place.device(x=3), place.device(c=1)
    mine, above, below, across = place.x, *(lax.rem(place.x + k, 4) for k in (1, 3, 2))
    shared = [copies.send(view(mine), view(mine), sibling)]
    first_up = copies.send(view(mine), view(mine), up)
    first_down = copies.send(view(mine), view(mine), down)
    half = ROWS // 2
    yield
    first_up.wait_recv()
    part = view(below).at[0:half]
    second_up = copies.send(part, part, up)
    shared.append(copies.send(view(below), view(below), sibling))
    yield
    first_down.wait_recv()
    part = view(above).at[half:ROWS]
    second_down = copies.send(part, part, down)
    shared.append(copies.send(view(above), view(above), sibling))
    yield
    second_up.wait_recv()
    part = view(across).at[0:half]
    shared.append(copies.send(part, part, sibling))
    yield
    second_down.wait_recv()
    part = view(across).at[half:ROWS]
    shared.append(copies.send(part, part, sibling))
    yield
    for copy in shared:
        copy.wait_recv()


def tokens_gather_kernel(block, tokens, send_sems, recv_sems, local_sem):
    place = Place()
    own = pltpu.make_async_copy(block, tokens.at[place.xh, place.c, place.t], local_sem)
    own.start()
    greet([place.device(x=1), place.device(x=3), place.device(c=1)])
    own.wait()
    copies = Copies(send_sems, recv_sems)
    run_all([gather_tokens_job(copies, place, tokens)])
    copies.finish()


def tokens_gather(block):
    return pl.pallas_call(
        tokens_gather_kernel,
        out_shape=jax.ShapeDtypeStruct((2, 2, 2, ROWS, WIDTH), BF16),
        in_specs=[pl.BlockSpec(memory_space=pl.ANY)],
        out_specs=pl.BlockSpec(memory_space=pl.ANY),
        scratch_shapes=[
            pltpu.SemaphoreType.DMA((9,)),
            pltpu.SemaphoreType.DMA((9,)),
            pltpu.SemaphoreType.DMA,
        ],
        compiler_params=pltpu.CompilerParams(collective_id=2, has_side_effects=True),
        name="tokens_gather",
    )(block).reshape(8 * ROWS, WIDTH)


def scatter_tokens_job(copies, place, parts, siblings, small, large):
    c = place.c
    mine, above, below, across = place.x, *(lax.rem(place.x + k, 4) for k in (1, 3, 2))

    def view(x, core):
        return parts.at[lax.div(x, 2), core, lax.rem(x, 2)]

    up, down, sibling = place.device(x=1), place.device(x=3), place.device(c=1)
    half = ROWS // 2
    shared = [copies.send(view(x, 1 - c), siblings.at[x], sibling) for x in (across, above, below, mine)]
    yield
    shared[0].wait_recv()
    add_blocks(view(across, c), siblings.at[across])
    first_up = copies.send(view(across, c).at[0:half], small.at[0], up)
    first_down = copies.send(view(across, c).at[half:ROWS], small.at[1], down)
    shared[1].wait_recv()
    add_blocks(view(above, c), siblings.at[above])
    shared[2].wait_recv()
    add_blocks(view(below, c), siblings.at[below])
    yield
    first_up.wait_recv()
    add_blocks(view(above, c).at[0:half], small.at[0])
    second_up = copies.send(view(above, c), large.at[0], up)
    yield
    first_down.wait_recv()
    add_blocks(view(below, c).at[half:ROWS], small.at[1])
    second_down = copies.send(view(below, c), large.at[1], down)
    shared[3].wait_recv()
    yield
    second_up.wait_recv()
    yield
    second_down.wait_recv()


def tokens_scatter_kernel(given, out, parts, siblings, small, large, send_sems, recv_sems, local_sem):
    place = Place()
    load = pltpu.make_async_copy(given, parts, local_sem)
    load.start()
    greet([place.device(x=1), place.device(x=3), place.device(c=1)])
    load.wait()
    copies = Copies(send_sems, recv_sems)
    run_all([scatter_tokens_job(copies, place, parts, siblings, small, large)])
    mine = parts.at[place.xh, place.c, place.t]
    other = siblings.at[place.x]

    def step(i, carry):
        rows = pl.ds(pl.multiple_of(i * 16, 16), 16)
        out[rows, :] = (
            mine[rows, :].astype(F32)
            + other[rows, :].astype(F32)
            + large[0, rows, :].astype(F32)
            + large[1, rows, :].astype(F32)
        )
        return carry

    lax.fori_loop(0, ROWS // 16, step, 0)
    copies.finish()


def tokens_scatter(parts):
    return pl.pallas_call(
        tokens_scatter_kernel,
        out_shape=jax.ShapeDtypeStruct((ROWS, WIDTH), F32),
        in_specs=[pl.BlockSpec(memory_space=pl.ANY)],
        out_specs=pl.BlockSpec(memory_space=pltpu.VMEM),
        scratch_shapes=[
            pltpu.VMEM((2, 2, 2, ROWS, WIDTH), BF16),
            pltpu.VMEM((4, ROWS, WIDTH), BF16),
            pltpu.VMEM((2, ROWS // 2, WIDTH), BF16),
            pltpu.VMEM((2, ROWS, WIDTH), BF16),
            pltpu.SemaphoreType.DMA((8,)),
            pltpu.SemaphoreType.DMA((8,)),
            pltpu.SemaphoreType.DMA,
        ],
        compiler_params=pltpu.CompilerParams(
            collective_id=3, has_side_effects=True, vmem_limit_bytes=32 * 2**20
        ),
        name="tokens_scatter",
    )(parts.reshape(2, 2, 2, ROWS, WIDTH))


def sum_everywhere_kernel(given, out, total, pair, rings, send_sems, recv_sems):
    place = Place()
    steps = [dict(c=1)]
    for axis in ("x", "y", "z"):
        steps += [{axis: k} for k in (1, 2, 3)]
    greet([place.device(**step) for step in steps])
    copies = Copies(send_sems, recv_sems)
    total[...] = given[...]
    copy = copies.send(total, pair, place.device(c=1))
    copy.wait_recv()
    copies.finish()
    total[...] = total[...] + pair[...]
    for k, axis in enumerate(("x", "y", "z")):
        mine = getattr(place, axis)
        rings[k, mine] = total[...]
        sent = [copies.send(total, rings.at[k, mine], place.device(**{axis: s})) for s in (1, 3, 2)]
        for copy in sent:
            copy.wait_recv()
        copies.finish()
        total[...] = (rings[k, 0] + rings[k, 1]) + (rings[k, 2] + rings[k, 3])
    out[...] = total[...]


def sum_everywhere(block):
    rows, columns = block.shape
    return pl.pallas_call(
        sum_everywhere_kernel,
        out_shape=jax.ShapeDtypeStruct(block.shape, F32),
        in_specs=[pl.BlockSpec(memory_space=pltpu.VMEM)],
        out_specs=pl.BlockSpec(memory_space=pltpu.VMEM),
        scratch_shapes=[
            pltpu.VMEM((rows, columns), F32),
            pltpu.VMEM((rows, columns), F32),
            pltpu.VMEM((3, 4, rows, columns), F32),
            pltpu.SemaphoreType.DMA((10,)),
            pltpu.SemaphoreType.DMA((10,)),
        ],
        compiler_params=pltpu.CompilerParams(collective_id=4, has_side_effects=True),
        name="sum_everywhere",
    )(block)


def norm_scale(values, gain):
    return values * lax.rsqrt(jnp.mean(values * values, axis=-1, keepdims=True) + EPSILON) * gain


def rotary(values, positions):
    half_size = values.shape[-1] // 2
    frequency = THETA ** (-2.0 * jnp.arange(half_size, dtype=jnp.float32) / values.shape[-1])
    angles = positions[:, None] * frequency[None, :]
    angles = jnp.concatenate([angles, angles], axis=-1)[:, None, :]
    rotated = jnp.concatenate([-values[..., half_size:], values[..., :half_size]], axis=-1)
    return values * jnp.cos(angles) + rotated * jnp.sin(angles)


def prepare(projected, gain, positions):
    head_size = gain.shape[0]
    shaped = projected.reshape(projected.shape[:-1] + (projected.shape[-1] // head_size, head_size))
    return rotary(norm_scale(shaped, gain), positions)


def swiglu(gate_proj, up_proj):
    return jax.nn.silu(gate_proj) * up_proj


def contract_rows(left_side, right_side):
    return lax.dot_general(
        left_side, right_side, (((0,), (0,)), ((), ())), preferred_element_type=jnp.float32
    )


def contract_cols(left_side, right_side):
    return lax.dot_general(
        left_side, right_side, (((1,), (1,)), ((), ())), preferred_element_type=jnp.float32
    )


def einsum(form, left_side, right_side):
    return jnp.einsum(form, left_side, right_side, preferred_element_type=jnp.float32)


def masked_scores(query_rot, key_rot, spans):
    rows = key_rot.shape[1]
    places = jnp.arange(rows, dtype=jnp.int32)
    allowed = (places[None, :] <= places[:, None])[None] & (places[None, None, :] < spans[:, None, None])
    scores = einsum("bqhd,bkd->bhqk", query_rot, key_rot) * (query_rot.shape[-1] ** (-0.5))
    return jnp.where(allowed[:, None], scores, -1e30)


def attend_forward(query_rot, key_rot, values, spans):
    scores = masked_scores(query_rot, key_rot, spans)
    row_max = jnp.max(scores, axis=-1, keepdims=True)
    weights_exp = jnp.exp(scores - row_max)
    row_total = jnp.sum(weights_exp, axis=-1, keepdims=True)
    probabilities = (weights_exp / row_total).astype(BF16)
    mixed = einsum("bhqk,bkd->bqhd", probabilities, values).astype(BF16)
    return mixed, row_max + jnp.log(row_total)


def attend_backward(query_rot, key_rot, values, mixed_grad, log_totals, spans):
    scaling = query_rot.shape[-1] ** (-0.5)
    probabilities = jnp.exp(masked_scores(query_rot, key_rot, spans) - log_totals)
    prob_grad = einsum("bqhd,bkd->bhqk", mixed_grad, values)
    row_delta = jnp.sum(prob_grad * probabilities, axis=-1, keepdims=True)
    score_grad = (probabilities * (prob_grad - row_delta)).astype(BF16)
    query_grad = einsum("bhqk,bkd->bqhd", score_grad, key_rot) * scaling
    key_grad = einsum("bhqk,bqhd->bkd", score_grad, query_rot) * scaling
    value_grad = einsum("bhqk,bqhd->bkd", probabilities.astype(BF16), mixed_grad)
    return query_grad, key_grad, value_grad


def quarters(weight):
    rows, columns = weight.shape
    return weight.reshape(rows, 4, columns // 4).transpose(1, 0, 2)


def whole(blocks):
    count, rows, columns = blocks.shape
    return blocks.transpose(1, 0, 2).reshape(rows, count * columns).astype(F32)


def local(
    residual_in,
    query_weight,
    key_weight,
    value_weight,
    output_weight,
    gate_weight,
    up_weight,
    down_weight,
    input_gain,
    post_gain,
    query_gain,
    key_gain,
    lengths,
    cotangent,
):
    place = Place()
    fsdp_index = lax.axis_index("fsdp")
    small = jnp.concatenate(
        [
            input_gain[:, None],
            post_gain[:, None],
            jnp.pad(query_gain, (0, 30))[:, None],
            jnp.pad(key_gain, (0, 30))[:, None],
            jnp.pad(lengths, (0, 31)).astype(BF16)[:, None],
            jnp.zeros((32, 123), BF16),
        ],
        axis=1,
    )
    packed = (
        jnp.concatenate(
            [
                quarters(query_weight),
                quarters(key_weight),
                quarters(value_weight),
                jnp.broadcast_to(small[None], (4, 32, 128)),
            ],
            axis=2,
        ),
        quarters(output_weight),
        jnp.concatenate([quarters(gate_weight), quarters(up_weight)], axis=2),
        quarters(down_weight),
    )
    first, output_full, gate_up_full, down_full = (
        w.reshape(WIDTH, w.shape[-1]) for w in weights_gather(packed)
    )
    qkv_full = first[:, :512]
    small_full = first[:, 512:520].astype(F32)
    gain_in, gain_post = small_full[:, 0], small_full[:, 1]
    by_owner = small_full.reshape(64, 32, 8)
    gain_query = by_owner[:, :2, 2].reshape(128)
    gain_key = by_owner[:, :2, 3].reshape(128)
    all_lengths = by_owner[:, 0, 4].astype(jnp.int32).reshape(4, 2, 4, 2)
    spans = lax.dynamic_index_in_dim(
        lax.dynamic_index_in_dim(all_lengths, place.z, 0, False), place.y, 1, False
    ).reshape(4)

    inputs = residual_in.astype(F32)
    normed_one = norm_scale(inputs, gain_in).astype(BF16)
    seq_in = tokens_gather(normed_one)
    positions = jnp.arange(256, dtype=F32)
    qkv = jnp.dot(seq_in, qkv_full, preferred_element_type=F32)
    query_proj = qkv[:, :256].reshape(4, 256, 256)
    key_proj = qkv[:, 256:384].reshape(4, 256, 128)
    values = qkv[:, 384:512].astype(BF16).reshape(4, 256, 128)
    query_rot = prepare(query_proj, gain_query, positions).astype(BF16)
    key_rot = prepare(key_proj, gain_key, positions).astype(BF16)[:, :, 0]
    mixed, log_totals = attend_forward(query_rot, key_rot, values, spans)
    attended = mixed.reshape(1024, 256)
    attn_sum = tokens_scatter(contract_cols(attended, output_full).astype(BF16))
    middle = inputs + attn_sum
    normed_two = norm_scale(middle, gain_post).astype(BF16)
    seq_mid = tokens_gather(normed_two)
    gate_up = jnp.dot(seq_mid, gate_up_full, preferred_element_type=F32)
    gate_proj, up_proj = gate_up[:, :768], gate_up[:, 768:]
    hidden_units = swiglu(gate_proj, up_proj).astype(BF16)
    ffn_sum = tokens_scatter(contract_cols(hidden_units, down_full).astype(BF16))
    block_out = (middle + ffn_sum).astype(BF16)

    rows_mine = place.t * ROWS + jnp.arange(ROWS, dtype=jnp.int32)
    grad_out = jnp.where((rows_mine < lengths[0])[:, None], cotangent.astype(F32), 0.0)
    ffn_grad = tokens_gather(grad_out.astype(BF16))
    down_grad = contract_rows(ffn_grad, hidden_units)
    hidden_grad = jnp.dot(ffn_grad, down_full, preferred_element_type=F32)
    unused_value, swiglu_pull = jax.vjp(swiglu, gate_proj, up_proj)
    gate_grad, up_grad = swiglu_pull(hidden_grad)
    gate_up_grad = jnp.concatenate([gate_grad.astype(BF16), up_grad.astype(BF16)], axis=1)
    gate_up_w_grad = contract_rows(seq_mid, gate_up_grad)
    mid_part = tokens_scatter(contract_cols(gate_up_grad, gate_up_full).astype(BF16))
    unused_mid, post_pull = jax.vjp(norm_scale, middle, gain_post)
    mid_grad, post_gain_part = post_pull(mid_part)
    mid_grad = grad_out + mid_grad
    proj_grad = tokens_gather(mid_grad.astype(BF16))
    output_w_grad = contract_rows(proj_grad, attended)
    attended_grad = jnp.dot(proj_grad, output_full, preferred_element_type=F32).astype(BF16)
    query_rot_grad, key_rot_grad, value_grad = attend_backward(
        query_rot, key_rot, values, attended_grad.reshape(4, 256, 2, 128), log_totals, spans
    )
    unused_query, query_pull = jax.vjp(
        lambda projected, gain: prepare(projected, gain, positions), query_proj, gain_query
    )
    query_grad, query_gain_part = query_pull(query_rot_grad)
    unused_key, key_pull = jax.vjp(
        lambda projected, gain: prepare(projected, gain, positions), key_proj, gain_key
    )
    key_grad, key_gain_part = key_pull(key_rot_grad[:, :, None])
    qkv_grad = jnp.concatenate(
        [
            query_grad.astype(BF16).reshape(1024, 256),
            key_grad.astype(BF16).reshape(1024, 128),
            value_grad.astype(BF16).reshape(1024, 128),
        ],
        axis=1,
    )
    qkv_w_grad = contract_rows(seq_in, qkv_grad)
    in_part = tokens_scatter(contract_cols(qkv_grad, qkv_full).astype(BF16))
    unused_in, in_pull = jax.vjp(norm_scale, inputs, gain_in)
    inputs_grad, in_gain_part = in_pull(in_part)
    input_grad = (mid_grad + inputs_grad).astype(BF16)
    down_out, gate_up_out, output_out, qkv_out = weights_scatter(
        [g.astype(BF16) for g in (down_grad, gate_up_w_grad, output_w_grad, qkv_w_grad)]
    )
    gain_sums = sum_everywhere(
        jnp.concatenate(
            [
                in_gain_part[None],
                post_gain_part[None],
                jnp.pad(query_gain_part, (0, WIDTH - 128))[None],
                jnp.pad(key_gain_part, (0, WIDTH - 128))[None],
                jnp.zeros((4, WIDTH), F32),
            ],
            axis=0,
        )
    )
    return (
        block_out,
        input_grad,
        whole(qkv_out[:, :, :256]),
        whole(qkv_out[:, :, 256:384]),
        whole(qkv_out[:, :, 384:]),
        whole(output_out),
        whole(gate_up_out[:, :, :768]),
        whole(gate_up_out[:, :, 768:]),
        whole(down_out),
        lax.dynamic_slice(gain_sums[0], (fsdp_index * 32,), (32,)),
        lax.dynamic_slice(gain_sums[1], (fsdp_index * 32,), (32,)),
        lax.dynamic_slice(gain_sums[2], (fsdp_index * 2,), (2,)),
        lax.dynamic_slice(gain_sums[3], (fsdp_index * 2,), (2,)),
    )


def solution(mesh):
    weights = P("fsdp", "tp")
    tokens = P(("fsdp", "tp"), None)
    vector = P("fsdp")
    return jax.shard_map(
        local,
        mesh=mesh,
        in_specs=(tokens,) + (weights,) * 7 + (vector,) * 5 + (tokens,),
        out_specs=(tokens,) * 2 + (weights,) * 7 + (vector,) * 4,
        check_vma=False,
    )
```

```python
import jax
import jax.numpy as jnp
from jax import lax
from jax.experimental import pallas as pl
from jax.experimental.pallas import tpu as pltpu
from jax.sharding import PartitionSpec as P

EPSILON = 1e-06
THETA = 1000000.0
MESH = pl.DeviceIdType.MESH
F32 = jnp.float32
BF16 = jnp.bfloat16
ROWS = 128
WIDTH = 2048
SPAN = 256
HEAD = 128
UNITS = 768
BLOCK = 256
SCALING = HEAD**-0.5


class Place:
    def __init__(self):
        index = lax.axis_index("fsdp")
        self.t = lax.axis_index("tp")
        self.c = lax.rem(index, 2)
        self.y = lax.rem(lax.div(index, 2), 4)
        self.xh = lax.rem(lax.div(index, 8), 2)
        self.z = lax.div(index, 16)
        self.x = self.xh * 2 + self.t

    def device(self, x=0, y=0, z=0, c=0):
        ax = lax.rem(self.x + x, 4) if x else self.x
        ay = lax.rem(self.y + y, 4) if y else self.y
        az = lax.rem(self.z + z, 4) if z else self.z
        ac = 1 - self.c if c else self.c
        return (((az * 2 + lax.div(ax, 2)) * 4 + ay) * 2 + ac, lax.rem(ax, 2))

    def around(self, mine):
        return tuple(lax.rem(mine + k, 4) for k in (1, 3, 2))


class Copies:
    def __init__(self, send_sems, recv_sems):
        self.send_sems, self.recv_sems = send_sems, recv_sems
        self.used = 0
        self.open = []

    def send(self, source, target, device):
        copy = pltpu.make_async_remote_copy(
            src_ref=source,
            dst_ref=target,
            send_sem=self.send_sems.at[self.used],
            recv_sem=self.recv_sems.at[self.used],
            device_id=device,
            device_id_type=MESH,
        )
        copy.start()
        self.used += 1
        self.open.append(copy)
        return copy

    def finish(self):
        for copy in self.open:
            copy.wait_send()
        self.open = []


class Job:
    def __init__(self, base, body):
        self.copies = Copies(base.send_sems, base.recv_sems)
        self.copies.used = base.used
        self.body = body(self.copies)
        self.base = base
        self.done = False

    def step(self, count=1):
        for _ in range(count):
            if not self.done:
                try:
                    next(self.body)
                except StopIteration:
                    self.done = True

    def drain(self):
        while not self.done:
            self.step()

    def close(self):
        self.drain()
        self.copies.finish()


def run_until(job, others=()):
    while not job.done:
        job.step()
        for other in others:
            other.step()


def greet(devices):
    barrier = pltpu.get_barrier_semaphore()
    for device in devices:
        pl.semaphore_signal(barrier, inc=1, device_id=device, device_id_type=MESH)
    pl.semaphore_wait(barrier, len(devices))


def both(*jobs):
    jobs = list(jobs)
    while jobs:
        alive = []
        for job in jobs:
            try:
                next(job)
                alive.append(job)
            except StopIteration:
                pass
        jobs = alive
        if jobs:
            yield


def ring_gather(copies, mine, view, halves, up, down):
    above, below = lax.rem(mine + 1, 4), lax.rem(mine + 3, 4)
    first_up = copies.send(view(mine), view(mine), up)
    first_down = copies.send(view(mine), view(mine), down)
    yield
    first_up.wait_recv()
    half = halves(below)[0]
    second_up = copies.send(half, half, up)
    first_down.wait_recv()
    half = halves(above)[1]
    second_down = copies.send(half, half, down)
    yield
    second_up.wait_recv()
    second_down.wait_recv()


def ring_scatter(copies, mine, view, halves, up, down, small, large):
    above, below, across = (lax.rem(mine + k, 4) for k in (1, 3, 2))
    first_up = copies.send(halves(across)[0], small[0], up)
    first_down = copies.send(halves(across)[1], small[1], down)
    yield
    first_up.wait_recv()
    add_blocks(halves(above)[0], small[0])
    second_up = copies.send(view(above), large[0], up)
    first_down.wait_recv()
    add_blocks(halves(below)[1], small[1])
    second_down = copies.send(view(below), large[1], down)
    yield
    second_up.wait_recv()
    second_down.wait_recv()


def add_blocks(target, *sources, rows=32):
    shape = target.shape
    depth = shape[-2] // rows
    count = depth
    for extent in shape[:-2]:
        count *= extent

    def step(i, carry):
        rest = lax.div(i, depth)
        index = []
        for extent in reversed(shape[:-2]):
            index.insert(0, lax.rem(rest, extent))
            rest = lax.div(rest, extent)
        index.append(pl.ds(pl.multiple_of(lax.rem(i, depth) * rows, rows), rows))
        index = tuple(index)
        total = target[index].astype(F32)
        for source in sources:
            total = total + source[index].astype(F32)
        target[index] = total.astype(target.dtype)
        return carry

    lax.fori_loop(0, count, step, 0)


def gather_weight(copies, place, sources, full):
    z, xh, y, c = place.z, place.xh, place.y, place.c
    rows = pl.ds(pl.multiple_of(c * 32, 32), 32)
    exchanged = []
    for take, columns in sources:
        spot = full.at[z, xh, y, rows, columns]
        exchanged += [
            copies.send(take(xh * 2 + 1 - c), spot, place.device(c=1)),
            copies.send(take((1 - xh) * 2 + c), spot, place.device(x=2)),
            copies.send(take((1 - xh) * 2 + 1 - c), spot, place.device(x=2, c=1)),
        ]
    yield
    for copy in exchanged:
        copy.wait_recv()
    z_up, z_down = place.device(z=1), place.device(z=3)
    y_up, y_down = place.device(y=1), place.device(y=3)
    yield from both(
        ring_gather(
            copies, y, lambda p: full.at[z, 0, p],
            lambda p: (full.at[z, 0, p, 0:32], full.at[z, 0, p, 32:64]), y_up, y_down,
        ),
        ring_gather(
            copies, z, lambda p: full.at[p, 1, y],
            lambda p: (full.at[p, 1, y, 0:32], full.at[p, 1, y, 32:64]), z_up, z_down,
        ),
    )
    yield from both(
        ring_gather(
            copies, z, lambda p: full.at[p, 0],
            lambda p: (full.at[p, 0, 0:2], full.at[p, 0, 2:4]), z_up, z_down,
        ),
        ring_gather(
            copies, y, lambda p: full.at[:, 1, p],
            lambda p: (full.at[0:2, 1, p], full.at[2:4, 1, p]), y_up, y_down,
        ),
    )


def scatter_weight(copies, place, full, land, stage, recv, columns):
    z, xh, y, c = place.z, place.xh, place.y, place.c
    small_a, small_b, large_a, large_b, small_c, small_d, large_c, large_d = (
        (r.at[0, ..., columns], r.at[1, ..., columns]) for r in recv
    )
    z_up, z_down = place.device(z=1), place.device(z=3)
    y_up, y_down = place.device(y=1), place.device(y=3)
    yield from both(
        ring_scatter(
            copies, z, lambda p: full.at[p, 0],
            lambda p: (full.at[p, 0, 0:2], full.at[p, 0, 2:4]), z_up, z_down, small_a, large_a,
        ),
        ring_scatter(
            copies, y, lambda p: full.at[:, 1, p],
            lambda p: (full.at[0:2, 1, p], full.at[2:4, 1, p]), y_up, y_down, small_b, large_b,
        ),
    )
    add_blocks(full.at[z, 0], *large_a)
    add_blocks(full.at[:, 1, y], *large_b)
    yield from both(
        ring_scatter(
            copies, y, lambda p: full.at[z, 0, p],
            lambda p: (full.at[z, 0, p, 0:32], full.at[z, 0, p, 32:64]), y_up, y_down, small_c, large_c,
        ),
        ring_scatter(
            copies, z, lambda p: full.at[p, 1, y],
            lambda p: (full.at[p, 1, y, 0:32], full.at[p, 1, y, 32:64]), z_up, z_down, small_d, large_d,
        ),
    )
    for half, large in ((0, large_c), (1, large_d)):
        for core in range(2):
            rows = slice(32 * core, 32 * core + 32)
            total = full[z, half, y, rows, :].astype(F32) + large[0][rows, :].astype(F32) + large[1][rows, :].astype(F32)
            stage[half, core] = total.astype(BF16)
    quarter = xh * 2 + c
    spot = land.at[quarter]
    exchanged = [
        copies.send(stage.at[xh, 1 - c], spot, place.device(c=1)),
        copies.send(stage.at[1 - xh, c], spot, place.device(x=2)),
        copies.send(stage.at[1 - xh, 1 - c], spot, place.device(x=2, c=1)),
    ]
    land[quarter] = stage[xh, c]
    yield
    for copy in exchanged:
        copy.wait_recv()


def gather_tokens(copies, place, tokens):
    c = place.c

    def view(x):
        return tokens.at[lax.div(x, 2), c, lax.rem(x, 2)]

    up, down, sibling = place.device(x=1), place.device(x=3), place.device(c=1)
    mine = place.x
    above, below, across = place.around(mine)
    half = ROWS // 2
    first_up = copies.send(view(mine), view(mine), up)
    first_down = copies.send(view(mine), view(mine), down)
    shared = [copies.send(view(mine), view(mine), sibling)]
    yield
    first_up.wait_recv()
    part = view(below).at[0:half]
    second_up = copies.send(part, part, up)
    shared.append(copies.send(view(below), view(below), sibling))
    first_down.wait_recv()
    part = view(above).at[half:ROWS]
    second_down = copies.send(part, part, down)
    shared.append(copies.send(view(above), view(above), sibling))
    yield
    second_up.wait_recv()
    part = view(across).at[0:half]
    shared.append(copies.send(part, part, sibling))
    second_down.wait_recv()
    part = view(across).at[half:ROWS]
    shared.append(copies.send(part, part, sibling))
    for copy in shared:
        copy.wait_recv()


def scatter_tokens(copies, place, parts, siblings, small, large):
    c = place.c
    mine = place.x
    above, below, across = place.around(mine)

    def view(x, core):
        return parts.at[lax.div(x, 2), core, lax.rem(x, 2)]

    up, down, sibling = place.device(x=1), place.device(x=3), place.device(c=1)
    half = ROWS // 2
    shared = [copies.send(view(x, 1 - c), siblings.at[x], sibling) for x in (across, above, below, mine)]
    yield
    shared[0].wait_recv()
    add_blocks(view(across, c), siblings.at[across])
    first_up = copies.send(view(across, c).at[0:half], small.at[0], up)
    first_down = copies.send(view(across, c).at[half:ROWS], small.at[1], down)
    shared[1].wait_recv()
    add_blocks(view(above, c), siblings.at[above])
    ahead_up = copies.send(view(above, c).at[half:ROWS], large.at[0, half:ROWS], up)
    shared[2].wait_recv()
    add_blocks(view(below, c), siblings.at[below])
    ahead_down = copies.send(view(below, c).at[0:half], large.at[1, 0:half], down)
    shared[3].wait_recv()
    yield
    first_up.wait_recv()
    add_blocks(view(above, c).at[0:half], small.at[0])
    second_up = copies.send(view(above, c).at[0:half], large.at[0, 0:half], up)
    first_down.wait_recv()
    add_blocks(view(below, c).at[half:ROWS], small.at[1])
    second_down = copies.send(view(below, c).at[half:ROWS], large.at[1, half:ROWS], down)
    yield
    ahead_up.wait_recv()
    ahead_down.wait_recv()
    second_up.wait_recv()
    second_down.wait_recv()


def sum_everywhere(copies, place, total, pair, rings):
    copy = copies.send(total, pair, place.device(c=1))
    yield
    copy.wait_recv()
    copies.finish()
    total[...] = total[...] + pair[...]
    for k, axis in enumerate(("x", "y", "z")):
        mine = getattr(place, axis)
        rings[k, mine] = total[...]
        sent = [copies.send(total, rings.at[k, mine], place.device(**{axis: s})) for s in (1, 3, 2)]
        yield
        for copy in sent:
            copy.wait_recv()
        copies.finish()
        total[...] = (rings[k, 0] + rings[k, 1]) + (rings[k, 2] + rings[k, 3])


def dot(left, right):
    return jnp.dot(left, right, preferred_element_type=F32)


def dot_cols(left, right):
    return lax.dot_general(left, right, (((1,), (1,)), ((), ())), preferred_element_type=F32)


def dot_rows(left, right):
    return lax.dot_general(left, right, (((0,), (0,)), ((), ())), preferred_element_type=F32)


def half_turn(values):
    return pltpu.roll(values, HEAD // 2, 1)


def scale_of(values):
    return lax.rsqrt(jnp.mean(values * values, axis=-1, keepdims=True) + EPSILON)


def columns_of(index, width=BLOCK, base=0):
    return pl.ds(pl.multiple_of(base + index * width, 128), width)


def over(count, body):
    def step(i, carry):
        body(i)
        return carry

    lax.fori_loop(0, count, step, 0)


def by_rows(count, body, rows=16):
    over(count // rows, lambda i: body(pl.ds(pl.multiple_of(i * rows, rows), rows)))


def fold(values):
    return jnp.sum(values.reshape(values.shape[0] // 8, 8, values.shape[1]), axis=0)


INPUTS = (
    "residual", "cotangent", "query_w", "key_w", "value_w", "output_w", "gate_w", "up_w", "down_w", "small", "cosine", "sine",
)
OUTPUTS = (
    "block_out", "input_grad", "query_out", "key_out", "value_out", "output_out", "gate_out", "up_out", "down_out", "gain_out",
    "kept",
)


def scratch():
    tokens = pltpu.VMEM((2, 2, 2, ROWS, WIDTH), BF16)
    shapes = {
        "tokens_a": tokens,
        "tokens_b": tokens,
        "tokens_c": tokens,
        "parts": tokens,
        "siblings": pltpu.VMEM((4, ROWS, WIDTH), BF16),
        "small_recv": pltpu.VMEM((2, ROWS // 2, WIDTH), BF16),
        "large_recv": pltpu.VMEM((2, ROWS, WIDTH), BF16),
        "small_full": pltpu.VMEM((4, 2, 4, 64, 256), BF16),
        "qkv": pltpu.VMEM((4, 2, 4, 64, 512), BF16),
        "out": pltpu.VMEM((4, 2, 4, 64, 256), BF16),
        "gate_up": pltpu.VMEM((4, 2, 4, 64, 2 * UNITS), BF16),
        "down": pltpu.VMEM((4, 2, 4, 64, UNITS), BF16),
        "down_grad": pltpu.VMEM((4, 2, 4, 64, UNITS), BF16),
    }
    for k in range(2):
        for n, extent in enumerate(((2, 2, 64), (2, 2, 64), (2, 4, 64), (2, 4, 64), (2, 32), (2, 32), (2, 64), (2, 64))):
            shapes[f"recv{k}{n}"] = pltpu.VMEM(extent + (UNITS,), BF16)
    for k in range(4):
        shapes[f"stage{k}"] = pltpu.VMEM((2, 2, 32, UNITS), BF16)
        shapes[f"land{k}"] = pltpu.VMEM((4, 32, UNITS), BF16)
    shapes |= {
        "query_pre": pltpu.VMEM((4, SPAN, 256), F32),
        "key_pre": pltpu.VMEM((4, SPAN, 128), F32),
        "value": pltpu.VMEM((4, SPAN, 128), BF16),
        "query_rot": pltpu.VMEM((4, SPAN, 256), BF16),
        "key_rot": pltpu.VMEM((4, SPAN, 128), BF16),
        "attended": pltpu.VMEM((4, SPAN, 256), BF16),
        "qkv_grad": pltpu.VMEM((4, SPAN, 512), BF16),
        "hidden": pltpu.VMEM((4, SPAN, UNITS), BF16),
        "gate_up_grad": pltpu.VMEM((4, SPAN, 2 * UNITS), BF16),
        "inputs": pltpu.VMEM((ROWS, WIDTH), BF16),
        "grads_in": pltpu.VMEM((ROWS, WIDTH), BF16),
        "middle": pltpu.VMEM((ROWS, WIDTH), F32),
        "mid_grad": pltpu.VMEM((ROWS, WIDTH), F32),
        "gains": pltpu.VMEM((16, WIDTH), F32),
        "vectors": pltpu.VMEM((16, 128), F32),
        "in_acc": pltpu.VMEM((8, WIDTH), F32),
        "post_acc": pltpu.VMEM((8, WIDTH), F32),
        "head_acc": pltpu.VMEM((16, 128), F32),
        "total": pltpu.VMEM((8, 640), F32),
        "pair": pltpu.VMEM((8, 640), F32),
        "rings": pltpu.VMEM((3, 4, 8, 640), F32),
        "send_sems": pltpu.SemaphoreType.DMA((300,)),
        "recv_sems": pltpu.SemaphoreType.DMA((300,)),
        "local_sems": pltpu.SemaphoreType.DMA((16,)),
        "free_tokens": pltpu.SemaphoreType.REGULAR,
        "free_weights": pltpu.SemaphoreType.REGULAR((2,)),
    }
    return shapes


class Refs:
    def __init__(self, names, refs):
        for name, ref in zip(names, refs, strict=True):
            setattr(self, name, ref)


def layer_kernel(*refs):
    r = Refs(INPUTS + OUTPUTS + tuple(scratch()), refs)
    place = Place()
    z, xh, y, c, t = place.z, place.xh, place.y, place.c, place.t
    quarter = xh * 2 + c
    base = Copies(r.send_sems, r.recv_sems)

    def job(count, body):
        made = Job(base, body)
        base.used += count
        return made

    def local(index, source, target):
        copy = pltpu.make_async_copy(source, target, r.local_sems.at[index])
        copy.start()
        return copy

    def taken(weight, width):
        return lambda q: weight.at[:, columns_of(q, width)]

    with jax.named_scope("entry"):
        own_rows = pl.ds(pl.multiple_of(c * 32, 32), 32)
        load_x = local(0, r.residual, r.tokens_a.at[xh, c, t])
        load_g = local(1, r.cotangent, r.tokens_c.at[xh, c, t])
        load_in = local(2, r.residual, r.inputs)
        plan = {
            "small": ([(lambda q: r.small, slice(0, 256))], r.small_full),
            "qkv": (
                [
                    (taken(r.query_w, 256), slice(0, 256)),
                    (taken(r.key_w, 128), slice(256, 384)),
                    (taken(r.value_w, 128), slice(384, 512)),
                ],
                r.qkv,
            ),
            "out": ([(taken(r.output_w, 256), slice(0, 256))], r.out),
            "down": ([(taken(r.down_w, UNITS), slice(0, UNITS))], r.down),
            "gate_up": (
                [(taken(r.gate_w, UNITS), slice(0, UNITS)), (taken(r.up_w, UNITS), slice(UNITS, 2 * UNITS))],
                r.gate_up,
            ),
        }
        loads = [load_g, load_in, local(3, r.cotangent, r.grads_in)]
        for sources, full in plan.values():
            for take, columns in sources:
                loads.append(local(len(loads) + 1, take(quarter), full.at[z, xh, y, own_rows, columns]))
        greet(
            [
                place.device(**step)
                for step in (
                    dict(c=1), dict(x=1), dict(x=3), dict(x=2), dict(x=2, c=1), dict(y=1), dict(y=3), dict(y=2), dict(z=1), dict(z=3), dict(z=2),
                )
            ]
        )
        load_x.wait()
        for copy in loads:
            copy.wait()
    weights = {}
    for name, (sources, full) in plan.items():
        weights[name] = job(
            3 * len(sources) + 16, lambda copies, s=sources, f=full: gather_weight(copies, place, s, f)
        )
    gather_x = job(9, lambda copies: gather_tokens(copies, place, r.tokens_a))
    with jax.named_scope("gather_x"):
        for name in ("small", "qkv", "out"):
            weights[name].step()
        gather_x.step()
        for name in ("down", "gate_up"):
            weights[name].step()
        weights["small"].step()
        for name in ("qkv", "out", "down", "gate_up"):
            weights["small"].step()
            weights[name].step()
        gather_x.step()
        weights["small"].drain()
        for name in ("qkv", "out", "down", "gate_up"):
            weights[name].step()
        gather_x.step()
        for name in ("qkv", "out"):
            weights[name].step()
        gather_x.drain()
        gather_x.close()

    with jax.named_scope("gains"):
        choose = (
            lax.broadcasted_iota(jnp.int32, (16, 128), 0) == lax.broadcasted_iota(jnp.int32, (16, 128), 1)
        ).astype(F32).astype(BF16)
        for k in range(8):
            rows = r.small_full[k // 2, k % 2, :, :, 0:128].reshape(BLOCK, 128)
            r.gains[:, BLOCK * k : BLOCK * (k + 1)] = dot_cols(choose, rows)
        r.vectors[...] = jnp.zeros((16, 128), F32)

        def add_vectors(i):
            for core in range(2):
                rows = r.small_full[lax.div(i, 8), lax.rem(lax.div(i, 4), 2), lax.rem(i, 4), 32 * core : 32 * core + 16, 128:256]
                r.vectors[...] = r.vectors[...] + rows.astype(F32)

        over(32, add_vectors)
        weights["small"].close()

    lanes = lax.broadcasted_iota(jnp.int32, (1, 128), 1)

    def length_of(s):
        owner = z * 16 + lax.div(s, 2) * 8 + y * 2 + lax.rem(s, 2)
        return jnp.sum(jnp.where(lanes == owner, r.vectors[2:3, :], 0.0), axis=-1, keepdims=True)

    def allowed(s):
        i = lax.broadcasted_iota(jnp.int32, (SPAN, SPAN), 0)
        j = lax.broadcasted_iota(jnp.int32, (SPAN, SPAN), 1)
        return (j <= i) & (j.astype(F32) < length_of(s))

    with jax.named_scope("mask"):
        own_length = length_of(quarter)
        grad_block = r.tokens_c.at[xh, c, t]

        def mask_rows(rows):
            position = t * ROWS + rows.start + lax.broadcasted_iota(jnp.int32, (16, 1), 0)
            keep = position.astype(F32) < own_length
            grad_block[rows, :] = jnp.where(keep, grad_block[rows, :].astype(F32), 0.0).astype(BF16)

        by_rows(ROWS, mask_rows)
    gather_g = job(9, lambda copies: gather_tokens(copies, place, r.tokens_c))
    gather_g.step()

    def seq(buffer, s):
        return buffer[lax.div(s, 2), lax.rem(s, 2)].reshape(SPAN, WIDTH)

    def store_parts(s, k, values):
        r.parts[lax.div(s, 2), lax.rem(s, 2), :, :, columns_of(k)] = values.astype(BF16).reshape(2, ROWS, BLOCK)

    def norm_rows(source, target, gain):
        def body(rows):
            values = source[rows, :].astype(F32)
            target[rows, :] = (values * scale_of(values) * r.gains[gain : gain + 1, :]).astype(BF16)

        by_rows(ROWS, body)

    def rotate(values, gain):
        normed = values * scale_of(values) * r.vectors[gain : gain + 1, :]
        return (normed * r.cosine[...] + half_turn(normed) * r.sine[...]).astype(BF16)

    def scores_of(s, head, mask):
        queries = r.query_rot[s, :, HEAD * head : HEAD * (head + 1)]
        return jnp.where(mask, dot_cols(queries, r.key_rot[s]) * SCALING, -1e30)

    def softmax(scores):
        powers = jnp.exp(scores - jnp.max(scores, axis=-1, keepdims=True))
        return powers / jnp.sum(powers, axis=-1, keepdims=True)

    def attention(s):
        for half in range(2):
            block = r.tokens_a.at[lax.div(s, 2), lax.rem(s, 2), half]
            norm_rows(block, block, 0)
        rows = seq(r.tokens_a, s)
        r.query_pre[s] = dot(rows, r.qkv[..., 0:256].reshape(WIDTH, 256))
        key_value = dot(rows, r.qkv[..., 256:512].reshape(WIDTH, 256))
        r.key_pre[s] = key_value[:, :128]
        r.value[s] = key_value[:, 128:].astype(BF16)
        for head in range(2):
            here = slice(HEAD * head, HEAD * (head + 1))
            r.query_rot[s, :, here] = rotate(r.query_pre[s, :, here], 0)
        r.key_rot[s] = rotate(r.key_pre[s], 1)
        mask = allowed(s)
        for head in range(2):
            weights_of = softmax(scores_of(s, head, mask)).astype(BF16)
            r.attended[s, :, HEAD * head : HEAD * (head + 1)] = dot(weights_of, r.value[s]).astype(BF16)

    def output_parts(s):
        over(
            8,
            lambda k: store_parts(
                s, k, dot_cols(r.attended[s], r.out[lax.div(k, 2), lax.rem(k, 2)].reshape(BLOCK, 256))
            ),
        )

    def order(i):
        return lax.rem(xh + lax.div(i, 2), 2) * 2 + lax.rem(c + i, 2)

    with jax.named_scope("attention"):
        weights["qkv"].drain()
        over(2, lambda i: attention(order(i)))
        for name in ("down", "gate_up"):
            weights[name].step()
        weights["out"].drain()
        over(2, lambda i: attention(order(i + 2)))
        gather_g.step()
        over(4, lambda i: output_parts(order(i)))
        keep = local(0, r.tokens_a, r.kept)

    def scatter_job():
        return job(
            10, lambda copies: scatter_tokens(copies, place, r.parts, r.siblings, r.small_recv, r.large_recv)
        )

    def scattered(rows):
        return (
            r.parts[xh, c, t, rows, :].astype(F32)
            + r.siblings[place.x, rows, :].astype(F32)
            + r.large_recv[0, rows, :].astype(F32)
            + r.large_recv[1, rows, :].astype(F32)
        )

    with jax.named_scope("scatter_attn"):
        keep.wait()
        scatter_attn = scatter_job()
        scatter_attn.step()
        scatter_attn.step()
        gather_g.drain()
        weights["down"].drain()
        scatter_attn.step()
        weights["gate_up"].step()
        scatter_attn.drain()

    with jax.named_scope("norm_two"):
        def second_norm(rows):
            values = r.inputs[rows, :].astype(F32) + scattered(rows)
            r.middle[rows, :] = values
            r.tokens_b[xh, c, t, rows, :] = (values * scale_of(values) * r.gains[1:2, :]).astype(BF16)

        by_rows(ROWS, second_norm)
        scatter_attn.close()
    gather_two = job(9, lambda copies: gather_tokens(copies, place, r.tokens_b))
    gather_two.step()

    def hidden_grad(s):
        rows = seq(r.tokens_c, s)
        over(
            3,
            lambda k: r.hidden.__setitem__(
                (s, slice(None), columns_of(k)),
                dot(rows, r.down[:, :, :, :, columns_of(k)].reshape(WIDTH, BLOCK)).astype(BF16),
            ),
        )

    with jax.named_scope("hidden_grad"):
        over(4, lambda i: hidden_grad(order(i)))
    with jax.named_scope("gather_two"):
        gather_two.step()
        weights["gate_up"].drain()
        gather_two.close()
        for name in ("qkv", "out", "down", "gate_up"):
            weights[name].close()
        gather_g.close()

    def feed_forward(s):
        rows = seq(r.tokens_b, s)

        def chunk(k):
            here, there = columns_of(k), columns_of(k, BLOCK, UNITS)
            gate = dot(rows, r.gate_up[:, :, :, :, here].reshape(WIDTH, BLOCK))
            up = dot(rows, r.gate_up[:, :, :, :, there].reshape(WIDTH, BLOCK))
            grad = r.hidden[s, :, here].astype(F32)
            sigmoid = 1.0 / (1.0 + jnp.exp(-gate))
            silu = gate * sigmoid
            r.hidden[s, :, here] = (silu * up).astype(BF16)
            r.gate_up_grad[s, :, here] = (grad * up * sigmoid * (1.0 + gate * (1.0 - sigmoid))).astype(BF16)
            r.gate_up_grad[s, :, there] = (grad * silu).astype(BF16)

        over(3, chunk)

    def mid_parts(s):
        def chunk(k):
            rows = r.gate_up[lax.div(k, 2), lax.rem(k, 2)].reshape(BLOCK, 2 * UNITS)
            grad = dot_cols(r.gate_up_grad[s], rows)
            store_parts(s, k, grad)
            here = columns_of(k)
            normed = r.tokens_b[lax.div(s, 2), lax.rem(s, 2), :, :, here].reshape(SPAN, BLOCK).astype(F32)
            r.post_acc[:, here] = r.post_acc[:, here] + fold(grad * normed)

        over(8, chunk)

    with jax.named_scope("feed_forward"):
        r.post_acc[...] = jnp.zeros((8, WIDTH), F32)
        over(4, lambda i: feed_forward(order(i)))
    with jax.named_scope("mid_parts"):
        over(4, lambda i: mid_parts(order(i)))

    zy = [place.device(**step) for step in (dict(y=1), dict(y=3), dict(z=1), dict(z=3))]

    def scatter_grad(full, index, slot, columns, wait, then):
        stage, land = getattr(r, f"stage{index}"), getattr(r, f"land{index}")
        recv = [getattr(r, f"recv{slot}{n}") for n in range(8)]

        def body(copies):
            if wait:
                pl.semaphore_wait(r.free_weights.at[slot], 4)
            inner = scatter_weight(
                copies, place, full, land.at[:, :, columns], stage.at[:, :, :, columns], recv, columns
            )
            while True:
                try:
                    next(inner)
                except StopIteration:
                    break
                yield
            if then:
                for device in zy:
                    pl.semaphore_signal(r.free_weights.at[slot], inc=1, device_id=device, device_id_type=MESH)

        return job(19, body)

    def weight_grad(buffer, factor, width, full, first=0):
        def chunk(k):
            rows = buffer[:, :, :, :, columns_of(k)].reshape(4 * SPAN, BLOCK)
            full[lax.div(k, 2), lax.rem(k, 2), :, :, first : first + width] = (
                dot_rows(rows, factor).astype(BF16).reshape(4, 64, width)
            )

        over(8, chunk)

    everything = slice(0, UNITS)
    scatter_down = scatter_grad(r.down_grad, 0, 0, everything, False, True)
    scatter_gate = scatter_grad(r.gate_up.at[:, :, :, :, 0:UNITS], 1, 1, everything, False, True)
    scatter_up = scatter_grad(r.gate_up.at[:, :, :, :, UNITS : 2 * UNITS], 2, 0, everything, True, False)
    scatter_out = scatter_grad(r.out, 3, 1, slice(0, 256), True, False)
    scatter_qkv = scatter_grad(r.qkv, 3, 1, slice(256, 768), False, False)

    scatter_mid = scatter_job()
    with jax.named_scope("down_grad"):
        scatter_mid.step()
        weight_grad(r.tokens_c, r.hidden[...].reshape(4 * SPAN, UNITS), UNITS, r.down_grad)
        scatter_mid.step()
        scatter_down.step()
    with jax.named_scope("gate_grad"):
        weight_grad(r.tokens_b, r.gate_up_grad[:, :, 0:UNITS].reshape(4 * SPAN, UNITS), UNITS, r.gate_up)
        scatter_gate.step()
        scatter_mid.step()
        scatter_down.step()
    with jax.named_scope("up_grad"):
        weight_grad(r.tokens_b, r.gate_up_grad[:, :, UNITS:].reshape(4 * SPAN, UNITS), UNITS, r.gate_up, UNITS)
        reload = local(1, r.kept, r.tokens_c)
        scatter_mid.drain()

    def norm_back(values, grad, gain):
        scale = scale_of(values)
        scaled = grad * gain
        return scale * scaled - values * (scale * scale * scale * jnp.mean(scaled * values, axis=-1, keepdims=True))

    with jax.named_scope("mid_grad"):
        def residual_grad(rows):
            position = t * ROWS + rows.start + lax.broadcasted_iota(jnp.int32, (16, 1), 0)
            keep_rows = position.astype(F32) < own_length
            outer = jnp.where(keep_rows, r.grads_in[rows, :].astype(F32), 0.0)
            grad = outer + norm_back(r.middle[rows, :], scattered(rows), r.gains[1:2, :])
            r.mid_grad[rows, :] = grad
            r.tokens_a[xh, c, t, rows, :] = grad.astype(BF16)

        by_rows(ROWS, residual_grad)
        scatter_mid.close()
    gather_h = job(9, lambda copies: gather_tokens(copies, place, r.tokens_a))
    gather_h.step()

    def ffn_parts(s):
        over(
            8,
            lambda k: store_parts(
                s, k, dot_cols(r.hidden[s], r.down[lax.div(k, 2), lax.rem(k, 2)].reshape(BLOCK, UNITS))
            ),
        )

    with jax.named_scope("ffn_parts"):
        over(4, ffn_parts)
        scatter_down.step()
        gather_h.step()
        scatter_gate.step()
        gather_h.drain()
        gather_h.close()
    scatter_ffn = scatter_job()
    scatter_ffn.step()

    def attention_back(s):
        rows = seq(r.tokens_a, s)
        grads = dot(rows, r.out[...].reshape(WIDTH, 256)).astype(BF16)
        mask = allowed(s)
        key_grad = jnp.zeros((SPAN, HEAD), F32)
        value_grad = jnp.zeros((SPAN, HEAD), F32)
        for head in range(2):
            here = slice(HEAD * head, HEAD * (head + 1))
            queries = r.query_rot[s, :, here]
            weights_of = softmax(scores_of(s, head, mask))
            head_grad = grads[:, here]
            weight_grads = dot_cols(head_grad, r.value[s])
            delta = jnp.sum(weight_grads * weights_of, axis=-1, keepdims=True)
            score_grad = (weights_of * (weight_grads - delta)).astype(BF16)
            query_grad = dot(score_grad, r.key_rot[s]) * SCALING
            key_grad = key_grad + dot_rows(score_grad, queries) * SCALING
            value_grad = value_grad + dot_rows(weights_of.astype(BF16), head_grad)
            r.qkv_grad[s, :, here] = head_back(r.query_pre[s, :, here], query_grad, 0).astype(BF16)
        r.qkv_grad[s, :, 256:384] = head_back(r.key_pre[s], key_grad, 1).astype(BF16)
        r.qkv_grad[s, :, 384:512] = value_grad.astype(BF16)

    def head_back(values, grad, gain):
        normed_grad = grad * r.cosine[...] - half_turn(grad) * r.sine[...]
        r.head_acc[8 * gain : 8 * gain + 8, :] = r.head_acc[8 * gain : 8 * gain + 8, :] + fold(
            normed_grad * values * scale_of(values)
        )
        return norm_back(values, normed_grad, r.vectors[gain : gain + 1, :])

    def in_parts(s):
        def chunk(k):
            grad = dot_cols(r.qkv_grad[s], r.qkv[lax.div(k, 2), lax.rem(k, 2)].reshape(BLOCK, 512))
            store_parts(s, k, grad)
            here = columns_of(k)
            normed = r.tokens_c[lax.div(s, 2), lax.rem(s, 2), :, :, here].reshape(SPAN, BLOCK).astype(F32)
            r.in_acc[:, here] = r.in_acc[:, here] + fold(grad * normed)

        over(8, chunk)

    with jax.named_scope("attention_back"):
        r.head_acc[...] = jnp.zeros((16, 128), F32)
        r.in_acc[...] = jnp.zeros((8, WIDTH), F32)
        over(2, lambda i: attention_back(order(i)))
        scatter_ffn.step()
        over(2, lambda i: attention_back(order(i + 2)))
        scatter_ffn.step()
        scatter_down.drain()
        scatter_up.step()
        reload.wait()
    with jax.named_scope("out_grad"):
        weight_grad(r.tokens_a, r.attended[...].reshape(4 * SPAN, 256), 256, r.out)
        scatter_ffn.drain()
    with jax.named_scope("block_out"):
        def block_rows(rows):
            r.block_out[rows, :] = (r.middle[rows, :] + scattered(rows)).astype(BF16)

        by_rows(ROWS, block_rows)
        scatter_ffn.close()
        partners = [place.device(c=1), place.device(x=1), place.device(x=3)]
        for device in partners:
            pl.semaphore_signal(r.free_tokens, inc=1, device_id=device, device_id_type=MESH)
    with jax.named_scope("in_parts"):
        over(4, in_parts)
        pl.semaphore_wait(r.free_tokens, 3)
        scatter_in = scatter_job()
        scatter_in.step()
        r.total[...] = jnp.zeros((8, 640), F32)
        for k in range(4):
            here = slice(512 * k, 512 * (k + 1))
            r.total[k : k + 1, 0:512] = jnp.sum(r.in_acc[:, here], axis=0, keepdims=True) / r.gains[0:1, here]
            r.total[4 + k : 5 + k, 0:512] = jnp.sum(r.post_acc[:, here], axis=0, keepdims=True) / r.gains[1:2, here]
        r.total[0:1, 512:640] = jnp.sum(r.head_acc[0:8, :], axis=0, keepdims=True)
        r.total[1:2, 512:640] = jnp.sum(r.head_acc[8:16, :], axis=0, keepdims=True)
        sum_gains = job(10, lambda copies: sum_everywhere(copies, place, r.total, r.pair, r.rings))
        scatter_in.step()
    with jax.named_scope("qkv_grad"):
        weight_grad(r.tokens_c, r.qkv_grad[...].reshape(4 * SPAN, 512), 512, r.qkv)
        scatter_in.step()
        scatter_gate.drain()
        scatter_out.step()
        scatter_qkv.step()
        sum_gains.step()
        scatter_up.step()
        sum_gains.step()
        scatter_out.step()
        scatter_qkv.step()
        sum_gains.step()
        scatter_in.drain()
    with jax.named_scope("input_grad"):
        def input_rows(rows):
            grad = norm_back(r.inputs[rows, :].astype(F32), scattered(rows), r.gains[0:1, :])
            r.input_grad[rows, :] = (r.mid_grad[rows, :] + grad).astype(BF16)

        by_rows(ROWS, input_rows)
    with jax.named_scope("last_scatters"):
        rest = [scatter_up, scatter_out, scatter_qkv, sum_gains]
        while not all(j.done for j in rest):
            for j in rest:
                j.step()
        r.gain_out[...] = r.total[...]
    with jax.named_scope("outputs"):
        for q in range(4):
            wide = slice(UNITS * q, UNITS * (q + 1))
            r.down_out[:, wide] = r.land0[q].astype(F32)
            r.gate_out[:, wide] = r.land1[q].astype(F32)
            r.up_out[:, wide] = r.land2[q].astype(F32)
            r.output_out[:, 256 * q : 256 * (q + 1)] = r.land3[q, :, 0:256].astype(F32)
            r.query_out[:, 256 * q : 256 * (q + 1)] = r.land3[q, :, 256:512].astype(F32)
            r.key_out[:, 128 * q : 128 * (q + 1)] = r.land3[q, :, 512:640].astype(F32)
            r.value_out[:, 128 * q : 128 * (q + 1)] = r.land3[q, :, 640:768].astype(F32)
    for made in (scatter_in, scatter_down, scatter_gate, scatter_up, scatter_out, scatter_qkv, sum_gains):
        made.close()


def rotation():
    frequency = THETA ** (-2.0 * jnp.arange(HEAD // 2, dtype=F32) / HEAD)
    angles = jnp.arange(SPAN, dtype=F32)[:, None] * frequency[None, :]
    sine = jnp.sin(angles)
    cosine = jnp.cos(angles)
    return jnp.concatenate([cosine, cosine], axis=1), jnp.concatenate([-sine, sine], axis=1)


def local(
    residual_in,
    query_weight,
    key_weight,
    value_weight,
    output_weight,
    gate_weight,
    up_weight,
    down_weight,
    input_gain,
    post_gain,
    query_gain,
    key_gain,
    lengths,
    cotangent,
):
    index = lax.axis_index("fsdp")
    lane = jnp.arange(128, dtype=jnp.int32)
    at_pair = lambda gain: jnp.where(lane == 2 * index, gain[0], jnp.where(lane == 2 * index + 1, gain[1], 0)).astype(BF16)
    vectors = jnp.stack([at_pair(query_gain), at_pair(key_gain), jnp.where(lane == index, lengths[0], 0).astype(BF16)])
    small = jnp.concatenate(
        [
            jnp.stack([input_gain, post_gain], axis=1),
            jnp.zeros((32, 126), BF16),
            jnp.concatenate([vectors, jnp.zeros((29, 128), BF16)], axis=0),
        ],
        axis=1,
    )
    cosine, sine = rotation()
    anywhere = pl.BlockSpec(memory_space=pl.ANY)
    vmem = pl.BlockSpec(memory_space=pltpu.VMEM)
    given = scratch()
    results = pl.pallas_call(
        layer_kernel,
        out_shape=[
            jax.ShapeDtypeStruct((ROWS, WIDTH), BF16),
            jax.ShapeDtypeStruct((ROWS, WIDTH), BF16),
            jax.ShapeDtypeStruct(query_weight.shape, F32),
            jax.ShapeDtypeStruct(key_weight.shape, F32),
            jax.ShapeDtypeStruct(value_weight.shape, F32),
            jax.ShapeDtypeStruct(output_weight.shape, F32),
            jax.ShapeDtypeStruct(gate_weight.shape, F32),
            jax.ShapeDtypeStruct(up_weight.shape, F32),
            jax.ShapeDtypeStruct(down_weight.shape, F32),
            jax.ShapeDtypeStruct((8, 640), F32),
            jax.ShapeDtypeStruct((2, 2, 2, ROWS, WIDTH), BF16),
        ],
        in_specs=[anywhere] * 9 + [vmem] * 3,
        out_specs=[vmem] * 10 + [anywhere],
        scratch_shapes=list(given.values()),
        compiler_params=pltpu.CompilerParams(
            collective_id=0, has_side_effects=True, vmem_limit_bytes=62 * 2**20
        ),
        name="layer",
    )(
        residual_in, cotangent, query_weight, key_weight, value_weight, output_weight, gate_weight, up_weight, down_weight,
        small, cosine, sine,
    )
    gains = results[9]
    return tuple(results[:9]) + (
        lax.dynamic_slice(gains[0:4, 0:512].reshape(WIDTH), (index * 32,), (32,)),
        lax.dynamic_slice(gains[4:8, 0:512].reshape(WIDTH), (index * 32,), (32,)),
        lax.dynamic_slice(gains[0, 512:640], (index * 2,), (2,)),
        lax.dynamic_slice(gains[1, 512:640], (index * 2,), (2,)),
    )


def solution(mesh):
    weights = P("fsdp", "tp")
    tokens = P(("fsdp", "tp"), None)
    vector = P("fsdp")
    return jax.shard_map(
        local,
        mesh=mesh,
        in_specs=(tokens,) + (weights,) * 7 + (vector,) * 5 + (tokens,),
        out_specs=(tokens,) * 2 + (weights,) * 7 + (vector,) * 4,
        check_vma=False,
    )
```
